256 devices in a mesh: seq: 64 (over z, y, core), mp: 4 (over x).
Axes of the slice: x: 4, y: 4, z: 8, core: 2. Of those that a mesh axis runs over, the one named last changes fastest.
Arguments:
- hidden: bfloat16 [65536, 4096], P('seq', 'mp')
- picked: int32 [8192], P('seq'), may hold values from 0 to 65535, as said below
- target: int32 [65536], P('seq'), may hold values from -1 to 8191, as said below
- norm_gain: bfloat16 [4096], replicated, may hold values from 0.099609375 to 1.8984375
- router_weight: bfloat16 [4096], replicated, may hold values from -0.1875 to 0.1875
- w_query: bfloat16 [4096, 2048], P('seq', 'mp')
- w_key: bfloat16 [4096, 2048], P('seq', 'mp')
- w_value: bfloat16 [4096, 2048], P('seq', 'mp'), may hold values from -0.1875 to 0.1875
- w_out: bfloat16 [2048, 4096], P(None, 'mp'), may hold values from -0.125 to 0.125
Outputs:
- mixed: bfloat16 [65536, 4096], P('seq', 'mp')
The draws below stay inside these ranges and needn't reach their ends.
Inputs may be any that keep to these rules, and one draw needn't show every extreme that they name: `picked`: entry g holds the position of the routed token of rank (g mod 128) * 64 + g div 128, ranks counting the 8192 routed positions in increasing order. target[p] = g where picked[g] = p, and -1 where p is not routed; each aligned block of 1024 positions holds at most 256 routed ones, and some block holds exactly 256.
All inputs are finite; a program needn't handle non-finite values.
Results may differ from the reference program's by a relative error of at most 0.004.
Values may be sent and summed in bfloat16 or wider, within the bound.
No kernel may reach another device: no remote copies, remote signals or barrier semaphores. Data moves between devices by JAX's collectives and lax.ppermute only.
A program may use at most 128 MiB of HBM per device.

```python
import math
import jax
import jax.numpy as jnp
from jax import lax

D = 4096
HEADS = 16
HEAD_DIM = 128
TOK_DEV = 1024
SOURCES = 64
SEL_DEV = 128
SEQ = 65536
SEL = 8192


def selection(key):
    first, second, third = jax.random.split(key, 3)
    half = SOURCES // 2
    order = jax.random.permutation(first, SOURCES)
    shifts = jax.random.randint(second, (half,), 0, SEL_DEV + 1)
    shifts = shifts.at[0].set(SEL_DEV)
    counts = jnp.full((SOURCES,), SEL_DEV, jnp.int32)
    counts = counts.at[order[:half]].add(shifts).at[order[half:2 * half]].add(-shifts)
    noise = jax.random.randint(third, (SOURCES, TOK_DEV), 0, 2 ** 20)
    scores = noise * TOK_DEV + jnp.arange(TOK_DEV, dtype=jnp.int32)[None, :]
    ordering = jnp.argsort(scores, axis=1)
    ranking = jnp.argsort(ordering, axis=1)
    chosen = (ranking < counts[:, None]).reshape(SEQ)
    rank = jnp.cumsum(chosen.astype(jnp.int32)) - 1
    compact = rank % SOURCES * SEL_DEV + rank // SOURCES
    target = jnp.where(chosen, compact, -1).astype(jnp.int32)
    spots = jnp.where(chosen, compact, SEL)
    picked = jnp.zeros((SEL,), jnp.int32).at[spots].set(jnp.arange(SEQ, dtype=jnp.int32), mode='drop')
    return (picked, target)


def shared_projection(key):
    return jax.random.normal(key, (D, HEADS * HEAD_DIM), jnp.float32)


def mixed_projection(common, key, shared_part, own_part):
    own = jax.random.normal(key, (D, HEADS * HEAD_DIM), jnp.float32)
    return ((shared_part * common + own_part * own) / math.sqrt(D)).astype(jnp.bfloat16)


def draw_picked(key, part):
    shared = selection(key)
    return shared[0]


def draw_target(key, part):
    shared = selection(key)
    return shared[1]


def draw_w_query(key, part):
    common = shared_projection(key)
    key = jax.random.fold_in(key, 2)
    return mixed_projection(common, key, 0.6, 0.8)


def draw_w_key(key, part):
    common = shared_projection(key)
    key = jax.random.fold_in(key, 3)
    return mixed_projection(common, key, 0.6, 0.8)


def draw_hidden(key, part):
    key = jax.random.fold_in(key, 5)
    first = jax.random.fold_in(key, 0)
    base = jax.random.normal(first, (SEQ, D), jnp.float32)
    return base.astype(jnp.bfloat16)


def level_of(stream_key, shape, pieces, low, high):
    def one(axis_at, parts):
        steps = jax.random.uniform(jax.random.fold_in(jax.random.fold_in(stream_key, 6), axis_at), (parts,), jnp.float32, low / len(pieces), high / len(pieces))
        return jnp.repeat(jnp.exp(steps), shape[axis_at] // parts).reshape((-1,) + (1,) * (len(shape) - axis_at - 1))

    factor_of = one(*pieces[0])
    for cut in pieces[1:]:
        factor_of = factor_of * one(*cut)
    return factor_of


def normal_values(key, shape, deviation, limit, cuts=(), kind=jnp.bfloat16):
    entries = deviation * jax.random.normal(key, shape, jnp.float32)
    if cuts:
        entries = entries * level_of(key, shape, cuts, -0.22, 0.18)
    return jnp.clip(entries, -limit, limit).astype(kind)


def setup_inputs(seed: int = 0) -> dict:
    key_list = jax.random.split(jax.random.key(seed), 10)
    return {
        "hidden": draw_hidden(jax.random.fold_in(key_list[9], 71), 0),
        "picked": draw_picked(jax.random.fold_in(key_list[9], 71), 0),
        "target": draw_target(jax.random.fold_in(key_list[9], 71), 0),
        "norm_gain": jnp.clip(1.0 + 0.18 * jax.random.normal(key_list[3], (D,), jnp.float32), 0.099609375, 1.8984375).astype(jnp.bfloat16),
        "router_weight": normal_values(key_list[4], (D,), (D // 4) ** -0.5, 0.1875),
        "w_query": draw_w_query(jax.random.fold_in(key_list[9], 71), 0),
        "w_key": draw_w_key(jax.random.fold_in(key_list[9], 71), 0),
        "w_value": normal_values(key_list[7], (D, HEADS * HEAD_DIM), (D // 4) ** -0.5, 0.1875, ((0, 64), (1, 4))),
        "w_out": normal_values(key_list[8], (HEADS * HEAD_DIM, D), (HEADS * HEAD_DIM) ** -0.5, 0.125, ((1, 4),)),
    }


def rotate(vec, positions):
    half = vec.shape[-1] // 2
    freq = jnp.exp(-math.log(10000.0) * (2.0 * jnp.arange(half, dtype=jnp.float32) / vec.shape[-1]))
    angle = positions.astype(jnp.float32)[:, None] * freq[None, :]
    cosine = jnp.cos(angle)[:, None, :]
    sine = jnp.sin(angle)[:, None, :]
    first = vec[..., :half]
    second = vec[..., half:]
    return jnp.concatenate([first * cosine - second * sine, second * cosine + first * sine], axis=-1)

def reference(hidden, picked, target, norm_gain, router_weight, w_query, w_key, w_value, w_out):
    rows = hidden[picked]
    whole = rows.astype(jnp.float32)
    inverse = lax.rsqrt(lax.optimization_barrier(jnp.mean(whole * whole, axis=-1, keepdims=True)) + 1e-05)
    normed = (whole * inverse * norm_gain.astype(jnp.float32)).astype(jnp.bfloat16)
    gate = jax.nn.sigmoid(jnp.dot(rows, router_weight, preferred_element_type=jnp.float32))
    query = jnp.dot(normed, w_query, preferred_element_type=jnp.float32).reshape(SEL, HEADS, HEAD_DIM)
    keys = jnp.dot(normed, w_key, preferred_element_type=jnp.float32).reshape(SEL, HEADS, HEAD_DIM)
    values = jnp.dot(normed, w_value, preferred_element_type=jnp.float32).reshape(SEL, HEADS, HEAD_DIM)
    query = rotate(query, picked).astype(jnp.bfloat16)
    keys = rotate(keys, picked).astype(jnp.bfloat16)
    values = values.astype(jnp.bfloat16)
    index = jnp.arange(SEL, dtype=jnp.int32)
    rank = index % SEL_DEV * SOURCES + index // SEL_DEV
    allowed = rank[None, :] <= rank[:, None]
    scale = 1.0 / math.sqrt(HEAD_DIM)

    def one_head(operands):
        head_q, head_k, head_v = operands
        scores = jnp.dot(head_q, head_k.T, preferred_element_type=jnp.float32) * scale
        scores = jnp.where(allowed, scores, -1e+30)
        top = lax.optimization_barrier(jnp.max(scores, axis=-1, keepdims=True))
        weights = jnp.where(allowed, jnp.exp(scores - top), 0.0)
        total = lax.optimization_barrier(jnp.sum(weights, axis=-1, keepdims=True))
        summed = jnp.dot(weights.astype(jnp.bfloat16), head_v, preferred_element_type=jnp.float32)
        return summed / total
    stacked = (jnp.moveaxis(query, 1, 0), jnp.moveaxis(keys, 1, 0), jnp.moveaxis(values, 1, 0))
    heads_out = lax.map(one_head, stacked)
    attended = jnp.moveaxis(heads_out, 0, 1).reshape(SEL, HEADS * HEAD_DIM).astype(jnp.bfloat16)
    update = jnp.dot(attended, w_out, preferred_element_type=jnp.float32)
    new_rows = (whole + gate[:, None] * update).astype(jnp.bfloat16)
    live = target >= 0
    taken = new_rows[jnp.where(live, target, 0).astype(jnp.int32)]
    return jnp.where(live[:, None], taken, hidden)
```

```python
import functools
import math

import jax
import jax.numpy as jnp
from jax import lax
from jax.experimental import pallas as pl
from jax.experimental.pallas import tpu as pltpu
from jax.sharding import Mesh, PartitionSpec as P

HEAD_DIM = 128
SEL_DEV = 128
NZ, NY, NC, NX = 8, 4, 2, 4
SHARDS = NZ * NY * NC
BUCKET = 4
BF16, F32, I32 = jnp.bfloat16, jnp.float32, jnp.int32
QSCALE = math.log2(math.e) / math.sqrt(HEAD_DIM)
NEG = -1e30


def project_kernel(rows_ref, w_ref, cos_ref, sin_ref, q_ref, kv_ref):
    acc = jnp.zeros((SEL_DEV, 3 * HEAD_DIM), F32)
    squares = jnp.zeros((SEL_DEV, 1), F32)
    for x in range(NX):
        piece = rows_ref[0, x]
        acc += jnp.dot(piece, w_ref[x * 1024 : (x + 1) * 1024, :], preferred_element_type=F32)
        wide = piece.astype(F32)
        squares += jnp.sum(wide * wide, axis=-1, keepdims=True)
    acc = acc * lax.rsqrt(squares * (1.0 / 4096) + 1e-05)
    cosine, sine = cos_ref[0], sin_ref[0]

    def turn(a):
        return a * cosine + pltpu.roll(a, 64, 1) * sine

    q_ref[0] = (turn(acc[:, :128]) * QSCALE).astype(BF16)
    kv_ref[0] = jnp.concatenate([turn(acc[:, 128:256]), acc[:, 256:]], axis=-1).astype(BF16)


def project(rows, w, cosine, sine):
    tile = lambda *tail: pl.BlockSpec((1,) + tail, lambda i: (i,) + (0,) * len(tail))
    return pl.pallas_call(
        project_kernel,
        grid=(NY,),
        in_specs=[
            tile(NX, SEL_DEV, 1024),
            pl.BlockSpec((4096, 384), lambda i: (0, 0)),
            tile(SEL_DEV, 128),
            tile(SEL_DEV, 128),
        ],
        out_specs=[tile(SEL_DEV, 128), tile(SEL_DEV, 256)],
        out_shape=[
            jax.ShapeDtypeStruct((NY, SEL_DEV, 128), BF16),
            jax.ShapeDtypeStruct((NY, SEL_DEV, 256), BF16),
        ],
        compiler_params=pltpu.CompilerParams(vmem_limit_bytes=32 << 20),
    )(rows, w, cosine, sine)


def attend_kernel(off_ref, q_ref, kv_ref, o_ref, qs, top, total, acc):
    for b in range(4):
        for y in range(NY):
            qs[b * 128 + y * 32 : b * 128 + y * 32 + 32] = q_ref[y, b * 32 : b * 32 + 32]
    top[...] = jnp.full(top.shape, NEG, F32)
    total[...] = jnp.zeros(total.shape, F32)
    acc[...] = jnp.zeros(acc.shape, F32)
    row = lax.broadcasted_iota(I32, (128, 512), 0)
    col = lax.broadcasted_iota(I32, (128, 512), 1)
    rank_q = row % 32 * 64 + row // 32 * 2 + off_ref[0]
    for b in range(4):
        live = slice(b * 128, 512)
        for part in range(4):
            block = kv_ref[part * 4 : part * 4 + 4, :, b * 32 : b * 32 + 32, :].reshape(512, 256)
            scores = lax.dot_general(
                qs[live], block[:, :128], (((1,), (1,)), ((), ())), preferred_element_type=F32
            )
            group = part * 4 + col // 128
            rank_k = col % 32 * 64 + col // 32 % 4 * 2 + group // 2 * 8 + group % 2
            edge = jnp.where(rank_k <= rank_q, scores[:128], NEG)
            scores = edge if b == 3 else jnp.concatenate([edge, scores[128:]], axis=0)
            old = top[live, :1]
            new = jnp.maximum(old, jnp.max(scores, axis=-1, keepdims=True))
            weights = jnp.exp2(scores - new)
            shrink = jnp.exp2(old - new)
            top[live] = jnp.broadcast_to(new, (512 - b * 128, 128))
            total[live] = total[live] * shrink + jnp.sum(weights, axis=-1, keepdims=True)
            acc[live] = acc[live] * shrink + jnp.dot(
                weights.astype(BF16), block[:, 128:], preferred_element_type=F32
            )
    done = (acc[...] / total[...]).astype(BF16)
    for b in range(4):
        for y in range(NY):
            o_ref[y, b * 32 : b * 32 + 32] = done[b * 128 + y * 32 : b * 128 + y * 32 + 32]


def attend(offset, query, keys_values):
    whole = pl.BlockSpec(memory_space=pltpu.VMEM)
    return pl.pallas_call(
        attend_kernel,
        in_specs=[pl.BlockSpec(memory_space=pltpu.SMEM), whole, whole],
        out_specs=whole,
        out_shape=jax.ShapeDtypeStruct((NY, SEL_DEV, 128), BF16),
        scratch_shapes=[
            pltpu.VMEM((512, 128), BF16),
            pltpu.VMEM((512, 128), F32),
            pltpu.VMEM((512, 128), F32),
            pltpu.VMEM((512, 128), F32),
        ],
        compiler_params=pltpu.CompilerParams(vmem_limit_bytes=32 << 20),
    )(offset, query, keys_values)


def around(array, axis, size):
    here = lax.axis_index(axis)
    got = [array] + [
        lax.ppermute(array, axis, [(i, (i + k) % size) for i in range(size)]) for k in range(1, size)
    ]
    stacked = jnp.stack(got)
    return stacked[(here - jnp.arange(size)) % size]


def per_device(hidden, picked, target, norm_gain, router_weight, w_query, w_key, w_value, w_out):
    z, y, c = lax.axis_index("z"), lax.axis_index("y"), lax.axis_index("c")
    shard = (z * NY + y) * NC + c

    gain = lax.dynamic_slice(norm_gain, (shard * 64,), (64,)).astype(F32)
    mine = jnp.concatenate(
        [w.reshape(64, NY, HEAD_DIM) for w in (w_query, w_key, w_value)], axis=-1
    ).transpose(1, 0, 2)
    mine = (mine.astype(F32) * gain[None, :, None]).astype(BF16)
    heads = lax.all_to_all(mine, "y", split_axis=0, concat_axis=0, tiled=True)
    weights = lax.all_gather(heads, ("z", "c"), axis=0, tiled=True)
    weights = weights.reshape(NZ, NC, NY, 64, 384).transpose(0, 2, 1, 3, 4).reshape(4096, 384)

    places = around(picked, "y", NY)
    half = HEAD_DIM // 2
    freq = jnp.exp(-math.log(10000.0) * (2.0 * jnp.arange(half, dtype=F32) / HEAD_DIM))
    angle = places.astype(F32)[..., None] * freq
    cosine, sine = jnp.cos(angle), jnp.sin(angle)
    cosine = jnp.concatenate([cosine, cosine], axis=-1)
    sine = jnp.concatenate([-sine, sine], axis=-1)

    live = target >= 0
    cell = jnp.where(live, target // SEL_DEV * BUCKET + target % BUCKET, -1)
    slots = jnp.arange(SHARDS * BUCKET, dtype=I32)
    pick_out = (cell[None, :] == slots[:, None]).astype(BF16)
    outgoing = jnp.dot(pick_out, hidden, preferred_element_type=F32).astype(BF16)
    arrived = lax.all_to_all(
        outgoing.reshape(SHARDS, BUCKET, -1), ("z", "y", "c"), split_axis=0, concat_axis=0, tiled=True
    ).reshape(SHARDS * BUCKET, -1)
    fetch = picked // hidden.shape[0] * BUCKET + jnp.arange(SEL_DEV, dtype=I32) % BUCKET
    pick_in = (fetch[:, None] == slots[None, :]).astype(BF16)
    own_rows = jnp.dot(pick_in, arrived, preferred_element_type=F32).astype(BF16)

    rows = lax.all_gather(own_rows, ("y", "x"), axis=0).reshape(NY, NX, SEL_DEV, 1024)
    query, mine_kv = project(rows, weights, cosine, sine)
    full = lax.dynamic_index_in_dim(rows, y, 0, keepdims=False)
    gate = jax.nn.sigmoid(
        jnp.einsum("xrf,xf->r", full, router_weight.reshape(NX, 1024), preferred_element_type=F32)
    )
    keys_values = lax.all_gather(mine_kv, ("z", "c"), axis=0)
    offset = (z * 8 + c).astype(I32).reshape(1)
    attended = attend(offset, query, keys_values)

    by_head = lax.all_to_all(attended, "y", split_axis=0, concat_axis=0, tiled=True)
    all_heads = lax.all_gather(by_head, "x", axis=0, tiled=True)
    flat = all_heads.transpose(1, 0, 2).reshape(SEL_DEV, 16 * HEAD_DIM)
    update = jnp.dot(flat, w_out, preferred_element_type=F32)
    new_rows = (own_rows.astype(F32) + gate[:, None] * update).astype(BF16)
    backward = jnp.dot(pick_in.T, new_rows, preferred_element_type=F32).astype(BF16)
    returned = lax.all_to_all(
        backward.reshape(SHARDS, BUCKET, -1), ("z", "y", "c"), split_axis=0, concat_axis=0, tiled=True
    ).reshape(SHARDS * BUCKET, -1)
    taken = jnp.dot(pick_out.T, returned, preferred_element_type=F32).astype(BF16)
    return jnp.where(live[:, None], taken, hidden)


def solution(mesh):
    cut = Mesh(mesh.devices.reshape(NZ, NY, NC, NX), ("z", "y", "c", "x"))
    seq = ("z", "y", "c")
    placed = (
        P(seq, "x"),
        P(seq),
        P(seq),
        P(),
        P(),
        P(seq, "x"),
        P(seq, "x"),
        P(seq, "x"),
        P(None, "x"),
    )
    return jax.shard_map(
        per_device, mesh=cut, in_specs=placed, out_specs=P(seq, "x"), check_vma=False
    )
```

```python
import functools
import math

import jax
import jax.numpy as jnp
from jax import lax
from jax.experimental import pallas as pl
from jax.experimental.pallas import tpu as pltpu
from jax.sharding import Mesh, PartitionSpec as P

HEAD_DIM = 128
SEL_DEV = 128
NZ, NY, NC, NX = 8, 4, 2, 4
SHARDS = NZ * NY * NC
BUCKET = 4
BF16, F32, I32 = jnp.bfloat16, jnp.float32, jnp.int32
QSCALE = math.log2(math.e) / math.sqrt(HEAD_DIM)
NEG = -1e30


def shift(array, axis, by, size):
    return lax.ppermute(array, axis, [(i, (i + by) % size) for i in range(size)])


def project_kernel(where_ref, over_x, over_y, far_a, far_b, w_ref, cos_ref, sin_ref, out_ref):
    z, y, c, x = (where_ref[i] for i in range(4))

    def rows(half, i):
        span = slice(half * 64, half * 64 + 64)
        got = [over_x[(x + i) & 3, span]]
        for r in range(1, NY):
            if i == 0:
                got.append(over_y[(y + r) & 3, span])
            elif half == 0:
                got.append(far_a[(y + r) & 3, i - 1])
            else:
                got.append(far_b[(x + i) & 3, r - 1])
        return jnp.concatenate(got, axis=0)

    def turn(a, cosine, sine):
        return a * cosine + pltpu.roll(a, 64, 1) * sine

    for half in range(2):
        span = slice(half * 64, half * 64 + 64)
        acc = jnp.zeros((256, 3 * HEAD_DIM), F32)
        squares = jnp.zeros((256, 128), F32)
        for i in range(NX):
            piece = rows(half, i)
            for j in range(2):
                away = ((((x + i) & 3) * 2 + j - z) * (1 - 2 * c)) & 7
                acc += jnp.dot(
                    piece[:, j * 512 : j * 512 + 512], w_ref[away], preferred_element_type=F32
                )
            for j in range(8):
                wide = piece[:, j * 128 : j * 128 + 128].astype(F32)
                squares += wide * wide
        mean = jnp.sum(squares, axis=-1, keepdims=True) * (1.0 / 4096)
        acc = acc * lax.rsqrt(mean + 1e-05)
        cosine = jnp.concatenate([cos_ref[(y + r) & 3, span] for r in range(NY)], axis=0)
        sine = jnp.concatenate([sin_ref[(y + r) & 3, span] for r in range(NY)], axis=0)
        key = turn(acc[:, 128:256], cosine, sine).astype(BF16)
        query = (turn(acc[:, :128], cosine, sine) * QSCALE).astype(BF16)
        out_ref[:, span, :128] = key.reshape(4, 64, 128)
        out_ref[:, span, 128:256] = acc[:, 256:].astype(BF16).reshape(4, 64, 128)
        out_ref[:, span, 256:] = query.reshape(4, 64, 128)


SCALARS = pl.BlockSpec(memory_space=pltpu.SMEM)
WHOLE = pl.BlockSpec(memory_space=pltpu.VMEM)
STATE = jax.ShapeDtypeStruct((2, 4, 128, 128), F32)


def project(where, pieces, w, cosine, sine):
    return pl.pallas_call(
        project_kernel,
        in_specs=[SCALARS] + [WHOLE] * 7,
        out_specs=WHOLE,
        out_shape=jax.ShapeDtypeStruct((NY, SEL_DEV, 384), BF16),
        compiler_params=pltpu.CompilerParams(vmem_limit_bytes=40 << 20),
        cost_estimate=pl.CostEstimate(flops=2 * 512 * 4096 * 384, bytes_accessed=8 << 20, transcendentals=512),
    )(where, *pieces, w, cosine, sine)


def attend_kernel(away, where_ref, kv_ref, own_ref, twin_ref, *refs):
    ins, outs = refs[:-2], refs[-2:]
    z, y, c = where_ref[0], where_ref[1], where_ref[2]
    cores = kv_ref.shape[0]
    row = lax.broadcasted_iota(I32, (256, 1), 0)
    rank_q = row % 32 * 64 + z * 8 + ((y + row // 32) & 3) * 2 + ((c + row // 128) & 1)
    col = lax.broadcasted_iota(I32, (1, cores * 128), 1)
    from_z = (z + away * (2 * c - 1)) & 7
    rank_k = col % 32 * 64 + from_z * 8 + ((y + col // 32) & 3) * 2 + ((c + col // 128) & 1)
    seen = rank_k <= rank_q

    def block(low, high, part):
        lanes = slice(part * 128, part * 128 + 128)
        return kv_ref[:, :, low:high, lanes].reshape(cores * 4 * (high - low), 128)

    def dot_t(a, b):
        return lax.dot_general(a, b, (((1,), (1,)), ((), ())), preferred_element_type=F32)

    for t in range(4):
        low, high = t * 32, t * 32 + 32
        query = jnp.concatenate(
            [r[:, low:high, 256:].reshape(128, 128) for r in (own_ref, twin_ref)], axis=0
        )
        edge = jnp.where(seen, dot_t(query, block(low, high, 0)), NEG)
        new = jnp.max(edge, axis=-1, keepdims=True)
        if t:
            past = dot_t(query, block(0, low, 0))
            new = jnp.maximum(new, jnp.max(past, axis=-1, keepdims=True))
        if ins:
            stats = jnp.concatenate([ins[0][1, t], ins[1][1, t]], axis=0)
            old = stats[:, :1]
            new = jnp.maximum(new, old)
        weights = jnp.exp2(edge - new)
        total = jnp.sum(weights, axis=-1, keepdims=True)
        acc = jnp.dot(weights.astype(BF16), block(low, high, 1), preferred_element_type=F32)
        if t:
            weights = jnp.exp2(past - new)
            total += jnp.sum(weights, axis=-1, keepdims=True)
            acc += jnp.dot(weights.astype(BF16), block(0, low, 1), preferred_element_type=F32)
        if ins:
            shrink = jnp.exp2(old - new)
            total += stats[:, 64:65] * shrink
            acc += jnp.concatenate([ins[0][0, t], ins[1][0, t]], axis=0) * shrink
        lane = lax.broadcasted_iota(I32, (256, 128), 1)
        stats = jnp.where(lane < 64, new, total)
        for half in range(2):
            outs[half][0, t] = acc[half * 128 : half * 128 + 128]
            outs[half][1, t] = stats[half * 128 : half * 128 + 128]


def attend(where, away, kv, own, twin, states):
    keys = kv.shape[0] * 512
    return pl.pallas_call(
        functools.partial(attend_kernel, away),
        in_specs=[SCALARS] + [WHOLE] * (3 + len(states)),
        out_specs=[WHOLE, WHOLE],
        out_shape=[STATE, STATE],
        compiler_params=pltpu.CompilerParams(vmem_limit_bytes=40 << 20),
        cost_estimate=pl.CostEstimate(
            flops=4 * 1024 * keys * 128, bytes_accessed=2 << 20, transcendentals=1024 * keys
        ),
    )(where, kv, own, twin, *states)


def merge_kernel(where_ref, mine_ref, other_ref, o_ref):
    y = where_ref[1]
    for t in range(4):
        mine, other = mine_ref[1, t], other_ref[1, t]
        top = jnp.maximum(mine[:, :1], other[:, :1])
        keep, add = jnp.exp2(mine[:, :1] - top), jnp.exp2(other[:, :1] - top)
        total = mine[:, 64:65] * keep + other[:, 64:65] * add
        done = ((mine_ref[0, t] * keep + other_ref[0, t] * add) / total).astype(BF16)
        for rel in range(4):
            to = (y + rel) & 3
            for x in range(NX):
                o_ref[to, x, t * 32 : t * 32 + 32, :] = done[rel * 32 : rel * 32 + 32]


def merge(where, mine, other):
    return pl.pallas_call(
        merge_kernel,
        in_specs=[SCALARS, WHOLE, WHOLE],
        out_specs=WHOLE,
        out_shape=jax.ShapeDtypeStruct((NY, NX, SEL_DEV, 128), BF16),
        compiler_params=pltpu.CompilerParams(vmem_limit_bytes=40 << 20),
    )(where, mine, other)


def spread(piece, axis):
    return lax.all_to_all(jnp.broadcast_to(piece[None], (4,) + piece.shape), axis, split_axis=0, concat_axis=0)


def rest(stack, here, span):
    return jnp.stack([lax.dynamic_index_in_dim(stack, (here + k) & 3, 0, keepdims=False)[span] for k in (1, 2, 3)])


def onward(array):
    pairs = [(z * NC, (z + 1) % NZ * NC) for z in range(NZ)]
    pairs += [(z * NC + 1, (z - 1) % NZ * NC + 1) for z in range(NZ)]
    return lax.ppermute(array, ("z", "c"), pairs)


def after(value, *others):
    return lax.optimization_barrier((value, *others))[0]


def per_device(hidden, picked, target, norm_gain, router_weight, w_query, w_key, w_value, w_out):
    z, y, c, x = (lax.axis_index(a).astype(I32) for a in ("z", "y", "c", "x"))
    shard = (z * NY + y) * NC + c
    where = jnp.stack([z, y, c, x])

    live = target >= 0
    cell = jnp.where(live, target // SEL_DEV * BUCKET + target % BUCKET, -1)
    slots = jnp.arange(SHARDS * BUCKET, dtype=I32)
    pick_out = (cell[None, :] == slots[:, None]).astype(BF16)
    outgoing = jnp.dot(pick_out, hidden, preferred_element_type=F32).astype(BF16)
    outgoing = outgoing.reshape(SHARDS, BUCKET, -1)
    arrived = lax.all_to_all(outgoing, ("z", "y", "c"), split_axis=0, concat_axis=0, tiled=True)
    arrived = arrived.reshape(SHARDS * BUCKET, -1)
    fetch = picked // hidden.shape[0] * BUCKET + jnp.arange(SEL_DEV, dtype=I32) % BUCKET
    pick_in = (fetch[:, None] == slots[None, :]).astype(BF16)
    own_rows = jnp.dot(pick_in, arrived, preferred_element_type=F32).astype(BF16)

    gain = lax.dynamic_slice(norm_gain, (shard * 64,), (64,)).astype(F32)[:, None]
    places = jnp.concatenate([picked // 256, picked % 256, jnp.zeros((128,), I32)]).astype(BF16)
    places = jnp.concatenate([places[None], jnp.zeros((15, 384), BF16)])
    w_query, w_key, w_value = (after(w, outgoing) for w in (w_query, w_key, w_value))

    def part(head):
        cut = [w[:, head * 128 : head * 128 + 128] for w in (w_query, w_key, w_value)]
        scaled = (jnp.concatenate(cut, axis=1).astype(F32) * gain).astype(BF16)
        return jnp.concatenate([scaled, places], axis=0)

    got = lax.all_to_all(jnp.stack([part(h) for h in range(NY)]), "y", split_axis=0, concat_axis=0)
    heads = got[:, :64]
    twin = shift(heads, "c", 1, NC)
    pair = jnp.stack([jnp.where(c == 0, heads, twin), jnp.where(c == 0, twin, heads)], axis=1)
    pair = after(pair, own_rows)
    ring = [pair]
    for _ in range(3):
        ring.append(onward(ring[-1]))
    ring.append(onward(lax.dynamic_index_in_dim(ring[-1], c, 1, keepdims=False)))
    mine = jnp.stack(ring[1:4])
    other = shift(jnp.concatenate([mine.reshape(3 * 512, 384), ring[4].reshape(256, 384)]), "c", 1, NC)
    last = other[1536:].reshape(NY, 64, 384)
    last = jnp.stack([jnp.where(c == 0, ring[4], last), jnp.where(c == 0, last, ring[4])], axis=1)
    weights = jnp.concatenate(
        [pair.reshape(512, 384)]
        + [other[:1536]]
        + [last.reshape(512, 384)]
        + [mine[k].reshape(512, 384) for k in (2, 1, 0)]
    ).reshape(NZ, 512, 384)

    places = got[:, 64, :].astype(F32)
    places = places[:, :128] * 256.0 + places[:, 128:256]
    half = HEAD_DIM // 2
    freq = jnp.exp(-math.log(10000.0) * (2.0 * jnp.arange(half, dtype=F32) / HEAD_DIM))
    angle = places[..., None] * freq
    cosine, sine = jnp.cos(angle), jnp.sin(angle)
    cosine = jnp.concatenate([cosine, cosine], axis=-1)
    sine = jnp.concatenate([-sine, sine], axis=-1)

    over_x, over_y = spread(own_rows, "x"), spread(own_rows, "y")
    far_a = spread(rest(over_x, x, slice(0, 64)), "y")
    far_b = spread(rest(over_y, y, slice(64, 128)), "x")
    qkv = project(where, [over_x, over_y, far_a, far_b], weights, cosine, sine)

    gate = jax.nn.sigmoid(
        jnp.einsum("xrf,xf->r", over_x, router_weight.reshape(NX, 1024), preferred_element_type=F32)
    )

    twin = shift(qkv, "c", 1, NC)
    near = onward(jnp.stack([qkv[:, :, :256], twin[:, :, :256]]))
    state = attend(where, 0, qkv[None], qkv, twin, [])
    next1, state = lax.optimization_barrier((onward(near), state))
    state = attend(where, 1, near, qkv, twin, state)
    next2, state = lax.optimization_barrier((onward(next1), state))
    state = attend(where, 2, next1, qkv, twin, state)
    far, state = lax.optimization_barrier((onward(next2[:1]), state))
    state = attend(where, 3, next2, qkv, twin, state)
    state = attend(where, 4, far, qkv, twin, state)
    ready = merge(where, state[0], shift(state[1], "c", 1, NC))

    by_head = lax.all_to_all(ready.reshape(16, SEL_DEV, 128), ("y", "x"), split_axis=0, concat_axis=0, tiled=True)
    flat = by_head.reshape(NY, NX, SEL_DEV, 128).transpose(2, 1, 0, 3).reshape(SEL_DEV, 16 * HEAD_DIM)
    update = jnp.dot(flat, w_out, preferred_element_type=F32)
    new_rows = (own_rows.astype(F32) + gate[:, None] * update).astype(BF16)
    backward = jnp.dot(pick_in.T, new_rows, preferred_element_type=F32).astype(BF16)
    returned = lax.all_to_all(
        backward.reshape(SHARDS, BUCKET, -1), ("z", "y", "c"), split_axis=0, concat_axis=0, tiled=True
    ).reshape(SHARDS * BUCKET, -1)
    taken = jnp.dot(pick_out.T, returned, preferred_element_type=F32).astype(BF16)
    return jnp.where(live[:, None], taken, hidden)


def solution(mesh):
    cut = Mesh(mesh.devices.reshape(NZ, NY, NC, NX), ("z", "y", "c", "x"))
    seq = ("z", "y", "c")
    placed = (
        P(seq, "x"),
        P(seq),
        P(seq),
        P(),
        P(),
        P(seq, "x"),
        P(seq, "x"),
        P(seq, "x"),
        P(None, "x"),
    )
    return jax.shard_map(
        per_device, mesh=cut, in_specs=placed, out_specs=P(seq, "x"), check_vma=False
    )
```
